256 devices in a mesh: col: 128 (over z, x, y), row: 2 (over core).
Axes of the slice: x: 4, y: 4, z: 8, core: 2. Of those that a mesh axis runs over, the one named last changes fastest.
Arguments:
- band_tiles: bfloat16 [2048, 5, 256, 256], P(('col', 'row')), may hold values from -0.125 to 0.125
- band_mask: int32 [2048, 5], P(('col', 'row')), may hold values from 0 to 1, as said below
- panels: bfloat16 [2, 2048, 256, 256], P(None, ('col', 'row')), may hold values from -6 to 6
- panel_seed: bfloat16 [2, 2048, 256, 256], P(None, ('col', 'row')), may hold values from -6 to 6
- diag_inverse: float32 [2, 256, 256], replicated, may hold values from -1.5 to 1.5, as said below
- cross_block: bfloat16 [256, 256], replicated, may hold values from -0.375 to 0.375
- cross_seed: float32 [256, 256], replicated, may hold values from -6 to 6
- diag_seed: float32 [256, 256], replicated, may hold values from -6 to 6
Outputs:
- panel_adjoint: bfloat16 [2, 2048, 256, 256], P(None, ('col', 'row'))
- cross_adjoint: float32 [256, 256], replicated
- diag_adjoint: float32 [256, 256], replicated
The draws below stay inside these ranges and needn't reach their ends.
Inputs may be any that keep to these rules, and one draw needn't show every extreme that they name: band_mask[c, 0] is 1 for every column c, and band_mask[c, d] is 0 where c + d >= 2048. Each diag_inverse[p] is lower triangular, with diagonal entries between 0.5 and 1.5.
All inputs are finite; a program needn't handle non-finite values.
Results may differ from the reference program's by a relative error of at most 0.0038.
Values may be sent and summed in bfloat16 or wider, within the bound.
A program may use at most 192 MiB of HBM per device.

```python
import math
import jax
import jax.numpy as jnp
from jax import lax

TILE = 256
PANEL_WIDTH = 256
BAND = 4
ROWS = 8
NT = 2048


def draw_band_mask(key, part):
    key = jax.random.fold_in(key, 11)
    level_key, full_key, bits_key = jax.random.split(key, 3)
    blocks = NT // ROWS
    levels = jax.random.randint(level_key, (blocks,), 1, 9)
    fullest = jax.random.randint(full_key, (), 0, blocks - 1)
    levels = jnp.where(jnp.arange(blocks) == fullest, 8, levels)
    column_level = jnp.repeat(levels, ROWS)
    random_bits = jax.random.randint(bits_key, (NT, BAND + 1), 0, 64)
    keeping = (random_bits < (column_level * column_level)[:, None]).astype(jnp.int32)
    columns = jnp.arange(NT)[:, None]
    offsets = jnp.arange(BAND + 1)[None, :]
    result = jnp.where(offsets == 0, 1, keeping)
    return jnp.where(columns + offsets < NT, result, 0).astype(jnp.int32)


def draw_diag_inverse(key, part):
    key = jax.random.fold_in(key, 23)
    lower_key, diag_key = jax.random.split(key, 2)
    width = PANEL_WIDTH
    spread = 0.6 / jnp.sqrt(jnp.float32(width))
    entries = jax.random.truncated_normal(lower_key, -4.0, 4.0, (2, width, width), jnp.float32) * spread
    diagonal = jax.random.uniform(diag_key, (2, width), jnp.float32, 0.5, 1.5)
    identity = jnp.eye(width, dtype=jnp.float32)
    return jnp.tril(entries, -1) + diagonal[:, :, None] * identity[None]


def level_of(key, shape, pieces, least, top_value):
    level, own = 1.0, jax.random.fold_in(key, 6)
    for axis_at, shards_of in pieces:
        draws = jnp.exp(jax.random.uniform(jax.random.fold_in(own, axis_at), (shards_of,), jnp.float32, least / len(pieces), top_value / len(pieces)))
        level = level * jnp.repeat(draws, shape[axis_at] // shards_of).reshape([-1 if axis == axis_at else 1 for axis in range(len(shape))])
    return level


def centred(key, dims, scale, most, pieces=(), held_as=jnp.bfloat16):
    gain = level_of(key, dims, pieces, -0.22, 0.18) if pieces else 1.0
    values = jax.random.normal(key, dims, jnp.float32) * scale * gain
    return jnp.minimum(jnp.maximum(values, -most), most).astype(held_as)


def setup_inputs(seed: int = 0) -> dict:
    keys = jax.random.split(jax.random.key(seed), 9)
    band_tiles = centred(keys[0], (NT, BAND + 1, TILE, TILE), (TILE * (2 * BAND + 1)) ** -0.5, 0.125, ((0, 256),))
    band_mask = draw_band_mask(jax.random.fold_in(keys[8], 71), 0)
    panels = centred(keys[2], (2, NT, TILE, PANEL_WIDTH), 1.0, 6.0, ((1, 256),))
    panel_seed = centred(keys[3], (2, NT, TILE, PANEL_WIDTH), 1.0, 6.0, ((1, 256),))
    diag_inverse = draw_diag_inverse(jax.random.fold_in(keys[8], 71), 0)
    cross_block = centred(keys[5], (PANEL_WIDTH, PANEL_WIDTH), PANEL_WIDTH ** -0.5, 0.375)
    cross_seed = centred(keys[6], (PANEL_WIDTH, PANEL_WIDTH), 1.0, 6.0, (), jnp.float32)
    diag_seed = centred(keys[7], (PANEL_WIDTH, PANEL_WIDTH), 1.0, 6.0, (), jnp.float32)
    return {"band_tiles": band_tiles, "band_mask": band_mask, "panels": panels, "panel_seed": panel_seed, "diag_inverse": diag_inverse, "cross_block": cross_block, "cross_seed": cross_seed, "diag_seed": diag_seed}


def reference(band_tiles, band_mask, panels, panel_seed, diag_inverse, cross_block, cross_seed, diag_seed):
    highest = lax.Precision.HIGHEST
    masked = band_tiles * band_mask[:, :, None, None].astype(jnp.bfloat16)
    panel_count = panels.shape[0]
    padding = jnp.zeros((panel_count, BAND, TILE, PANEL_WIDTH), jnp.bfloat16)
    below_rows = jnp.concatenate([panels, padding], axis=1).astype(jnp.float32)
    panel_rows = panels.astype(jnp.float32)
    upper_term = jnp.zeros((panel_count, NT, TILE, PANEL_WIDTH), jnp.float32)
    lower_term = jnp.zeros((panel_count, NT + BAND, TILE, PANEL_WIDTH), jnp.float32)
    for offset in range(BAND + 1):
        slot_tiles = masked[:, offset].astype(jnp.float32)
        upper_term = upper_term + jnp.einsum('cab,pcak->pcbk', slot_tiles, below_rows[:, offset:offset + NT])
        if offset > 0:
            lower_term = lower_term.at[:, offset:offset + NT].add(jnp.einsum('cab,pcbk->pcak', slot_tiles, panel_rows))
    band_term = upper_term + lower_term[:, :NT]
    scale_factor = 1.0 / math.sqrt(NT * TILE)
    adjoint_one = jnp.einsum('rbk,kl->rbl', panel_seed[1].astype(jnp.float32) - band_term[1], diag_inverse[1], precision=highest)
    zero_rows = panel_rows[0]
    cross_total = jnp.einsum('rbk,rbl->kl', adjoint_one, zero_rows, precision=highest) * scale_factor
    cross_adjoint = jnp.dot(cross_seed - cross_total, diag_inverse[0], precision=highest)
    cross_wide = cross_block.astype(jnp.float32)
    carried = jnp.einsum('rbk,kl->rbl', adjoint_one, cross_wide, precision=highest)
    adjoint_zero = jnp.einsum('rbk,kl->rbl', panel_seed[0].astype(jnp.float32) - band_term[0] - carried, diag_inverse[0], precision=highest)
    diag_total = jnp.einsum('rbk,rbl->kl', adjoint_zero, zero_rows, precision=highest) * scale_factor
    diag_adjoint = diag_seed - jnp.dot(cross_adjoint.T, cross_wide, precision=highest) - diag_total
    panel_adjoint = jnp.stack([adjoint_zero, adjoint_one]).astype(jnp.bfloat16)
    return (panel_adjoint, cross_adjoint, diag_adjoint)
```

```python
import functools
import math

import jax
import jax.numpy as jnp
from jax import lax
from jax.experimental import pallas as pl
from jax.experimental.pallas import tpu as pltpu
from jax.sharding import PartitionSpec as P

MESH = pl.DeviceIdType.MESH
F32 = jnp.float32
BF16 = jnp.bfloat16
TILE = 256
WIDE = 512
ROWS = 8
BAND = 4
PLANE_COLS = 16


def dot(a, b):
    return jnp.dot(a, b, preferred_element_type=F32)


def dot_t(a, b):
    return lax.dot_general(a, b, (((0,), (0,)), ((), ())), preferred_element_type=F32)


def exact_dot(a, b):
    return jnp.dot(a, b, precision=lax.Precision.HIGHEST, preferred_element_type=F32)


def split(a):
    high = a.astype(BF16)
    return high, (a - high.astype(F32)).astype(BF16)


def kernel(
    n_col,
    plane_cols,
    scale,
    band_hbm,
    mask,
    panels_hbm,
    seed_hbm,
    diag_inverse,
    cross_block,
    cross_seed,
    diag_seed,
    out_hbm,
    cross_out,
    diag_out,
    tiles,
    rows,
    seeds,
    acc,
    resid,
    left_in,
    total,
    staged,
    got_a,
    got_b,
    got_c,
    mine,
    w_high,
    w_low,
    out_v,
    in_sem,
    halo_send,
    halo_recv,
    part_send,
    part_recv,
    ar_send,
    ar_recv,
    out_sem,
):
    col, row = lax.axis_index("col"), lax.axis_index("row")
    n_dev = 2 * n_col
    index = col * 2 + row
    left, right = lax.rem(index + n_dev - 1, n_dev), lax.rem(index + 1, n_dev)
    left_id = (left // 2, lax.rem(left, 2))
    right_id = (right // 2, lax.rem(right, 2))
    n_a = 2 * plane_cols
    n_b = n_col // plane_cols
    depth, place = col // plane_cols, lax.rem(col, plane_cols)
    me_a = place * 2 + row

    def plane_id(step):
        peer = lax.rem(me_a + step, n_a)
        return peer, (depth * plane_cols + peer // 2, lax.rem(peer, 2))

    def line_id(step):
        return (lax.rem(depth + step, n_b) * plane_cols + place, row)

    def load(source, target, slot):
        copy = pltpu.make_async_copy(source, target, in_sem.at[slot])
        copy.start()
        return copy

    upper, lower = pl.ds(4, 4), pl.ds(0, 4)
    first, second = pl.ds(0, TILE), pl.ds(TILE, TILE)
    loads_hi = [
        load(panels_hbm.at[0, upper], rows.at[upper, :, first], 0),
        load(panels_hbm.at[1, upper], rows.at[upper, :, second], 1),
        load(band_hbm.at[upper], tiles.at[upper], 2),
    ]
    loads_lo = [
        load(panels_hbm.at[0, lower], rows.at[lower, :, first], 3),
        load(panels_hbm.at[1, lower], rows.at[lower, :, second], 4),
        load(band_hbm.at[lower], tiles.at[lower], 5),
        load(seed_hbm.at[0], seeds.at[:, :, first], 6),
        load(seed_hbm.at[1], seeds.at[:, :, second], 7),
    ]

    barrier = pltpu.get_barrier_semaphore()
    pl.semaphore_signal(barrier, inc=1, device_id=left_id, device_id_type=MESH)
    pl.semaphore_signal(barrier, inc=1, device_id=right_id, device_id_type=MESH)

    @pl.loop(1, n_a)
    def _(step):
        pl.semaphore_signal(barrier, inc=1, device_id=plane_id(step)[1], device_id_type=MESH)

    @pl.loop(1, n_b)
    def _(step):
        pl.semaphore_signal(barrier, inc=1, device_id=line_id(step), device_id_type=MESH)

    pl.semaphore_wait(barrier, n_a + n_b)

    halos = []
    for p, lanes in ((0, first), (1, second)):
        halos.append(
            pltpu.make_async_remote_copy(
                src_ref=panels_hbm.at[p, lower],
                dst_ref=rows.at[pl.ds(8, 4), :, lanes],
                send_sem=halo_send.at[p],
                recv_sem=halo_recv.at[p],
                device_id=left_id,
                device_id_type=MESH,
            )
        )
        halos[-1].start()

    def tile(c, d):
        keep = jnp.full((TILE, TILE), mask[c, d].astype(F32), F32).astype(BF16)
        return tiles[c, d] * keep

    def lower_terms(r, slots):
        lhs = jnp.concatenate([tile(r - d, d) for d in slots], axis=1)
        rhs = rows[pl.ds(r - slots[0], len(slots))].reshape(len(slots) * TILE, WIDE)
        return dot(lhs, rhs)

    def upper_terms(i, slots):
        lhs = jnp.concatenate([tile(i, d) for d in slots], axis=0)
        rhs = rows[pl.ds(i + slots[0], len(slots))].reshape(len(slots) * TILE, WIDE)
        return dot_t(lhs, rhs)

    for copy in loads_hi:
        copy.wait()
    parts = []
    for r in (11, 10, 9, 8):
        slots = list(range(4, r - 8, -1))
        resid[r] = (-lower_terms(r, slots)).astype(BF16)
        parts.append(
            pltpu.make_async_remote_copy(
                src_ref=resid.at[r],
                dst_ref=left_in.at[r - 8],
                send_sem=part_send.at[r - 8],
                recv_sem=part_recv.at[r - 8],
                device_id=right_id,
                device_id_type=MESH,
            )
        )
        parts[-1].start()

    inverse_zero, inverse_one = diag_inverse[0], diag_inverse[1]
    cross_wide = cross_block[...].astype(F32)
    through = exact_dot(inverse_one, cross_wide)
    carry = -exact_dot(through, inverse_zero)
    zeros = jnp.zeros((TILE, TILE), F32)
    weights = jnp.concatenate(
        [
            jnp.concatenate([inverse_zero, zeros], axis=1),
            jnp.concatenate([carry, inverse_one], axis=1),
        ],
        axis=0,
    )
    w_high[...], w_low[...] = split(weights)
    cross_base = exact_dot(cross_seed[...], inverse_zero)
    cross_out[...] = cross_base
    diag_out[...] = diag_seed[...] - exact_dot(cross_base.T, cross_wide)

    for copy in loads_lo:
        copy.wait()

    @pl.loop(4, 8)
    def _(i):
        acc[i] = seeds[i].astype(F32) - lower_terms(i, [4, 3, 2, 1])

    total[...] = jnp.zeros_like(total)

    for i in range(4):
        value = seeds[i].astype(F32)
        if i:
            value = value - lower_terms(i, list(range(i, 0, -1)))
        acc[i] = value

    @pl.loop(0, 4)
    def _(i):
        value = acc[i] - upper_terms(i, [0, 1, 2, 3, 4])
        acc[i] = value
        total[...] += dot_t(rows[i, :, :TILE], value.astype(BF16))

    for i in range(4, 8):
        acc[i] = acc[i] - upper_terms(i, list(range(0, 8 - i)))

    for copy in halos:
        copy.wait_recv()
    for i in range(4, 8):
        value = acc[i] - upper_terms(i, list(range(8 - i, 5)))
        resid[i] = value.astype(BF16)

    @pl.loop(4, 12)
    def _(i):
        total[...] += dot_t(rows[i, :, :TILE], resid[i])

    part_rows = WIDE // n_a
    for p in range(2):
        half = total[:, p * TILE : (p + 1) * TILE].astype(BF16)
        staged[pl.ds(p * n_a // 2, n_a // 2)] = half.reshape(n_a // 2, part_rows, TILE)

    @pl.loop(1, n_a)
    def _(step):
        peer, peer_id = plane_id(step)
        pltpu.make_async_remote_copy(
            src_ref=staged.at[peer],
            dst_ref=got_a.at[me_a],
            send_sem=ar_send.at[0],
            recv_sem=ar_recv.at[0],
            device_id=peer_id,
            device_id_type=MESH,
        ).start()

    got_a[me_a] = staged[me_a]

    def solve_rows(begin, end):
        @pl.loop(begin, end)
        def _(i):
            value = resid[i]
            one = value[:, TILE:]
            low, high = w_low, w_high
            zero_term = dot(value, high[:, :TILE]) + dot(value, low[:, :TILE])
            one_term = dot(one, high[TILE:, TILE:]) + dot(one, low[TILE:, TILE:])
            out_v[0, i] = zero_term.astype(BF16)
            out_v[1, i] = one_term.astype(BF16)

        copies = [
            pltpu.make_async_copy(
                out_v.at[p, pl.ds(begin, end - begin)],
                out_hbm.at[p, pl.ds(begin, end - begin)],
                out_sem.at[p, begin // 4],
            )
            for p in range(2)
        ]
        for copy in copies:
            copy.start()
        return copies

    outs = solve_rows(4, 8)

    def wait_bytes(buffer, count, send, recv):
        view = buffer.at[pl.ds(0, count)]
        pltpu.make_async_copy(view, view, recv).wait()
        pltpu.make_async_copy(view, view, send).wait()

    wait_bytes(got_a, n_a - 1, ar_send.at[0], ar_recv.at[0])
    mine[...] = jnp.sum(got_a[...].astype(F32), axis=0).astype(BF16)

    @pl.loop(1, n_b)
    def _(step):
        pltpu.make_async_remote_copy(
            src_ref=mine,
            dst_ref=got_b.at[depth],
            send_sem=ar_send.at[1],
            recv_sem=ar_recv.at[1],
            device_id=line_id(step),
            device_id_type=MESH,
        ).start()

    got_b[depth] = mine[...]

    for copy in parts:
        copy.wait_recv()

    @pl.loop(0, 4)
    def _(i):
        resid[i] = (acc[i] + left_in[i].astype(F32)).astype(BF16)

    wait_bytes(got_b, n_b - 1, ar_send.at[1], ar_recv.at[1])
    got_c[me_a] = jnp.sum(got_b[...].astype(F32), axis=0).astype(BF16)

    @pl.loop(1, n_a)
    def _(step):
        pltpu.make_async_remote_copy(
            src_ref=got_c.at[me_a],
            dst_ref=got_c.at[me_a],
            send_sem=ar_send.at[2],
            recv_sem=ar_recv.at[2],
            device_id=plane_id(step)[1],
            device_id_type=MESH,
        ).start()

    outs += solve_rows(0, 4)

    wait_bytes(got_c, n_a - 1, ar_send.at[2], ar_recv.at[2])
    zero_sum = got_c[pl.ds(0, n_a // 2)].reshape(TILE, TILE)
    one_sum = got_c[pl.ds(n_a // 2, n_a // 2)].reshape(TILE, TILE).astype(F32)
    inverse_zero, inverse_one = diag_inverse[0], diag_inverse[1]
    turned = exact_dot(one_sum, inverse_one).T
    cross_out[...] -= scale * exact_dot(turned, inverse_zero)
    mixed = exact_dot(one_sum, exact_dot(inverse_one, cross_block[...].astype(F32)))
    inner = mixed + mixed.T - zero_sum.astype(F32).T
    diag_out[...] += scale * exact_dot(inverse_zero.T, inner)

    for copy in halos + parts:
        copy.wait_send()
    for copy in outs:
        copy.wait()


def body(band_tiles, band_mask, panels, panel_seed, diag_inverse, cross_block, cross_seed, diag_seed):
    n_col = lax.axis_size("col")
    plane_cols = min(PLANE_COLS, n_col // 2)
    n_a, n_b = 2 * plane_cols, n_col // plane_cols
    part = (WIDE // n_a, TILE)
    scale = 1.0 / math.sqrt(2 * n_col * ROWS * TILE)
    any_spec = pl.BlockSpec(memory_space=pl.ANY)
    vmem = pl.BlockSpec(memory_space=pltpu.VMEM)
    smem = pl.BlockSpec(memory_space=pltpu.SMEM)
    dma = pltpu.SemaphoreType.DMA
    return tuple(
        pl.pallas_call(
            functools.partial(kernel, n_col, plane_cols, scale),
            out_shape=(
                jax.ShapeDtypeStruct(panels.shape, BF16),
                jax.ShapeDtypeStruct((TILE, TILE), F32),
                jax.ShapeDtypeStruct((TILE, TILE), F32),
            ),
            in_specs=[any_spec, smem, any_spec, any_spec, vmem, vmem, vmem, vmem],
            out_specs=(any_spec, vmem, vmem),
            scratch_shapes=[
                pltpu.VMEM((ROWS, BAND + 1, TILE, TILE), BF16),
                pltpu.VMEM((ROWS + BAND, TILE, WIDE), BF16),
                pltpu.VMEM((ROWS, TILE, WIDE), BF16),
                pltpu.VMEM((ROWS, TILE, WIDE), F32),
                pltpu.VMEM((ROWS + BAND, TILE, WIDE), BF16),
                pltpu.VMEM((BAND, TILE, WIDE), BF16),
                pltpu.VMEM((TILE, WIDE), F32),
                pltpu.VMEM((n_a,) + part, BF16),
                pltpu.VMEM((n_a,) + part, BF16),
                pltpu.VMEM((n_b,) + part, BF16),
                pltpu.VMEM((n_a,) + part, BF16),
                pltpu.VMEM(part, BF16),
                pltpu.VMEM((WIDE, WIDE), BF16),
                pltpu.VMEM((WIDE, WIDE), BF16),
                pltpu.VMEM((2, ROWS, TILE, TILE), BF16),
                dma((8,)),
                dma((2,)),
                dma((2,)),
                dma((BAND,)),
                dma((BAND,)),
                dma((3,)),
                dma((3,)),
                dma((2, 2)),
            ],
            compiler_params=pltpu.CompilerParams(
                collective_id=0, has_side_effects=True, vmem_limit_bytes=56 * 1024 * 1024
            ),
        )(band_tiles, band_mask, panels, panel_seed, diag_inverse, cross_block, cross_seed, diag_seed)
    )


def solution(mesh):
    split_rows = P(("col", "row"), None, None, None)
    split_panels = P(None, ("col", "row"), None, None)
    return jax.shard_map(
        body,
        mesh=mesh,
        in_specs=(split_rows, P(("col", "row"), None), split_panels, split_panels, P(), P(), P(), P()),
        out_specs=(split_panels, P(), P()),
        check_vma=False,
    )
```

```python
import functools
import math

import jax
import jax.numpy as jnp
from jax import lax
from jax.experimental import pallas as pl
from jax.experimental.pallas import tpu as pltpu
from jax.sharding import PartitionSpec as P

MESH = pl.DeviceIdType.MESH
F32 = jnp.float32
BF16 = jnp.bfloat16
TILE = 256
WIDE = 512
ROWS = 8
BAND = 4
PLANE_COLS = 16


def dot(a, b):
    return jnp.dot(a, b, preferred_element_type=F32)


def dot_t(a, b):
    return lax.dot_general(a, b, (((0,), (0,)), ((), ())), preferred_element_type=F32)


def split(a):
    high = a.astype(BF16)
    return high, (a - high.astype(F32)).astype(BF16)


def dot_three(a, b):
    (a_high, a_low), (b_high, b_low) = split(a), split(b)
    return dot(jnp.concatenate([a_high, a_high, a_low], axis=1), jnp.concatenate([b_high, b_low, b_high], axis=0))


def kernel(
    n_col,
    plane_cols,
    scale,
    band_hbm,
    mask_hbm,
    panels_hbm,
    seed_hbm,
    inverse_hbm,
    cross_hbm,
    cross_seed_hbm,
    diag_seed_hbm,
    out_v,
    cross_out,
    diag_out,
    tiles,
    rows,
    seeds,
    acc,
    resid,
    negm,
    left_in,
    total,
    staged,
    got_a,
    got_b,
    got_c,
    mine,
    w_zero,
    w_one,
    w_last,
    d_zero,
    mask,
    diag_inverse,
    cross_block,
    cross_seed,
    diag_seed,
    in_sem,
    halo_send,
    halo_recv,
    part_send,
    part_recv,
    ar_send,
    ar_recv,
):
    col, row = lax.axis_index("col"), lax.axis_index("row")
    n_dev = 2 * n_col
    index = col * 2 + row
    left, right = lax.rem(index + n_dev - 1, n_dev), lax.rem(index + 1, n_dev)
    left_id = (left // 2, lax.rem(left, 2))
    right_id = (right // 2, lax.rem(right, 2))
    n_a = 2 * plane_cols
    n_b = n_col // plane_cols
    depth, place = col // plane_cols, lax.rem(col, plane_cols)
    me_a = place * 2 + row

    side = math.isqrt(plane_cols) if math.isqrt(plane_cols) ** 2 == plane_cols else 1
    width = plane_cols // side
    moves = [(dx, dy, dc) for dx in range(side) for dy in range(width) for dc in range(2)][1:]
    moves.sort(key=lambda m: -min(m[0], side - m[0]) - min(m[1], width - m[1]))

    def plane_id(move):
        dx, dy, dc = move
        peer_x = lax.rem(place // width + dx, side)
        peer_place = peer_x * width + lax.rem(lax.rem(place, width) + dy, width)
        peer_row = lax.rem(row + dc, 2)
        return peer_place * 2 + peer_row, (depth * plane_cols + peer_place, peer_row)

    line_steps = sorted(range(1, n_b), key=lambda k: -min(k, n_b - k))

    def line_id(step):
        return (lax.rem(depth + step, n_b) * plane_cols + place, row)

    barrier = pltpu.get_barrier_semaphore()
    pl.semaphore_signal(barrier, inc=1, device_id=left_id, device_id_type=MESH)
    pl.semaphore_signal(barrier, inc=1, device_id=right_id, device_id_type=MESH)

    def load(source, target, slot):
        copy = pltpu.make_async_copy(source, target, in_sem.at[slot])
        copy.start()
        return copy

    upper, lower = pl.ds(4, 4), pl.ds(0, 4)
    first, second = pl.ds(0, TILE), pl.ds(TILE, TILE)
    loads_hi = [
        load(mask_hbm, mask, 8),
        load(panels_hbm.at[0, upper], rows.at[upper, :, first], 0),
        load(panels_hbm.at[1, upper], rows.at[upper, :, second], 1),
        load(band_hbm.at[upper], tiles.at[upper], 2),
    ]

    for step in range(1, n_b):
        pl.semaphore_signal(barrier, inc=1, device_id=line_id(step), device_id_type=MESH)
    for move in moves:
        pl.semaphore_signal(barrier, inc=1, device_id=plane_id(move)[1], device_id_type=MESH)

    loads_lo = [
        load(panels_hbm.at[0, lower], rows.at[lower, :, first], 3),
        load(panels_hbm.at[1, lower], rows.at[lower, :, second], 4),
        load(band_hbm.at[lower], tiles.at[lower], 5),
        load(seed_hbm.at[0], seeds.at[:, :, first], 6),
        load(seed_hbm.at[1], seeds.at[:, :, second], 7),
    ]
    loads_last = [
        load(inverse_hbm, diag_inverse, 9),
        load(cross_hbm, cross_block, 10),
        load(cross_seed_hbm, cross_seed, 11),
        load(diag_seed_hbm, diag_seed, 12),
    ]

    def tile(c, d):
        keep = jnp.full((TILE, TILE), mask[c, d].astype(F32), F32).astype(BF16)
        return tiles[c, d] * keep

    def lower_terms(r, slots):
        lhs = jnp.concatenate([tile(r - d, d) for d in slots], axis=1)
        rhs = rows[pl.ds(r - slots[0], len(slots))].reshape(len(slots) * TILE, WIDE)
        return dot(lhs, rhs)

    def upper_terms(i, slots):
        lhs = jnp.concatenate([tile(i, d) for d in slots], axis=0)
        rhs = rows[pl.ds(i + slots[0], len(slots))].reshape(len(slots) * TILE, WIDE)
        return dot_t(lhs, rhs)

    halos = []
    for begin in (0, 2):
        for p, lanes in ((0, first), (1, second)):
            halos.append(
                pltpu.make_async_remote_copy(
                    src_ref=panels_hbm.at[p, pl.ds(begin, 2)],
                    dst_ref=rows.at[pl.ds(8 + begin, 2), :, lanes],
                    send_sem=halo_send.at[p, begin // 2],
                    recv_sem=halo_recv.at[p, begin // 2],
                    device_id=left_id,
                    device_id_type=MESH,
                )
            )
    parts = []
    for begin in (2, 0):
        parts.append(
            pltpu.make_async_remote_copy(
                src_ref=resid.at[pl.ds(8 + begin, 2)],
                dst_ref=left_in.at[pl.ds(begin, 2)],
                send_sem=part_send.at[begin // 2],
                recv_sem=part_recv.at[begin // 2],
                device_id=right_id,
                device_id_type=MESH,
            )
        )

    pl.semaphore_wait(barrier, n_a + n_b)
    halos[0].start()
    halos[1].start()

    for copy in loads_hi:
        copy.wait()
    for r in (11, 10):
        resid[r] = (-lower_terms(r, list(range(4, r - 8, -1)))).astype(BF16)
    parts[0].start()
    for r in (9, 8):
        resid[r] = (-lower_terms(r, list(range(4, r - 8, -1)))).astype(BF16)

    def own_terms(i, slots):
        value = seeds[i].astype(F32)
        turned = -dot(tile(i, 0), rows[i, :, :TILE])
        if slots:
            terms = lower_terms(i, slots)
            value = value - terms
            turned = turned - terms[:, :TILE]
        acc[i] = value
        resid[i] = value.astype(BF16)
        negm[i] = turned.astype(BF16)

    def sum_over(i):
        lhs = jnp.concatenate([rows[i, :, :TILE], negm[i]], axis=0)
        rhs = jnp.concatenate([resid[i], rows[i]], axis=0)
        return dot_t(lhs, rhs)

    for copy in loads_lo:
        copy.wait()
    total[...] = jnp.zeros_like(total)

    @pl.loop(4, 8)
    def _(i):
        own_terms(i, [4, 3, 2, 1])
        total[...] += sum_over(i)

    for i in range(4):
        own_terms(i, list(range(i, 0, -1)))

    @pl.loop(0, 2)
    def _(i):
        total[...] += sum_over(i)

    parts[0].wait_recv()
    for i in (2, 3):
        arrived = left_in[i].astype(F32)
        value = acc[i] + arrived
        acc[i] = value
        resid[i] = value.astype(BF16)
        negm[i] = (negm[i].astype(F32) + arrived[:, :TILE]).astype(BF16)

    @pl.loop(2, 4)
    def _(i):
        total[...] += sum_over(i)

    halos[0].wait_recv()
    halos[1].wait_recv()
    for i in (8, 9):
        lhs = jnp.concatenate([rows[i, :, :TILE], resid[i, :, :TILE]], axis=0)
        rhs = jnp.concatenate([resid[i], rows[i]], axis=0)
        total[...] += dot_t(lhs, rhs)

    part_rows = WIDE // n_a
    for p in range(2):
        half = total[:, p * TILE : (p + 1) * TILE].astype(BF16)
        staged[pl.ds(p * n_a // 2, n_a // 2)] = half.reshape(n_a // 2, part_rows, TILE)

    for move in moves:
        peer, peer_id = plane_id(move)
        pltpu.make_async_remote_copy(
            src_ref=staged.at[peer],
            dst_ref=got_a.at[me_a],
            send_sem=ar_send.at[0],
            recv_sem=ar_recv.at[0],
            device_id=peer_id,
            device_id_type=MESH,
        ).start()

    halos[2].start()
    halos[3].start()
    parts[1].start()
    got_a[me_a] = staged[me_a]

    def wait_bytes(buffer, count, send, recv):
        view = buffer.at[pl.ds(0, count)]
        pltpu.make_async_copy(view, view, recv).wait()
        pltpu.make_async_copy(view, view, send).wait()

    for copy in loads_last:
        copy.wait()

    zero_high, zero_low = split(diag_inverse[0])
    one_high, one_low = split(diag_inverse[1])
    cross = cross_block[...]
    crosses = jnp.concatenate([cross, cross], axis=0)
    through = dot(jnp.concatenate([one_high, one_low], axis=1), crosses)
    through_high, through_low = split(through)
    carry_high, carry_low = split(-dot_three(through, diag_inverse[0]))
    w_zero[...] = jnp.concatenate([zero_high, carry_high, zero_low, carry_low], axis=0)
    w_one[...] = jnp.concatenate([one_high, one_low], axis=0)
    w_last[:TILE] = jnp.concatenate([one_high, through_high], axis=1)
    w_last[TILE:] = jnp.concatenate([one_low, through_low], axis=1)
    d_zero[...] = jnp.concatenate([zero_high, zero_low, zero_high], axis=0)
    base = dot_three(cross_seed[...], diag_inverse[0])
    cross_out[...] = base
    diag_out[...] = diag_seed[...] - dot_t(jnp.concatenate(split(base), axis=0), crosses)

    @pl.loop(0, 4)
    def _(i):
        acc[i] = acc[i] - upper_terms(i, [0, 1, 2, 3, 4])

    def solve(begin):
        value = resid[pl.ds(begin, 2)].reshape(2 * TILE, WIDE)
        one = value[:, TILE:]
        zero_term = dot(jnp.concatenate([value, value], axis=1), w_zero[...])
        one_term = dot(jnp.concatenate([one, one], axis=1), w_one[...])
        for p, term in ((0, zero_term), (1, one_term)):
            out_v[p, pl.ds(begin, 2)] = term.astype(BF16).reshape(2, TILE, TILE)

    resid[pl.ds(2, 2)] = acc[pl.ds(2, 2)].astype(BF16)
    solve(2)

    wait_bytes(got_a, n_a - 1, ar_send.at[0], ar_recv.at[0])
    mine[...] = jnp.sum(got_a[...].astype(F32), axis=0).astype(BF16)

    for step in line_steps:
        pltpu.make_async_remote_copy(
            src_ref=mine,
            dst_ref=got_b.at[depth],
            send_sem=ar_send.at[1],
            recv_sem=ar_recv.at[1],
            device_id=line_id(step),
            device_id_type=MESH,
        ).start()

    got_b[depth] = mine[...]

    @pl.loop(4, 6)
    def _(i):
        resid[i] = (acc[i] - upper_terms(i, [0, 1, 2, 3, 4])).astype(BF16)

    solve(4)
    acc[6] = acc[6] - upper_terms(6, [0, 1, 2, 3])
    acc[7] = acc[7] - upper_terms(7, [0, 1, 2])

    wait_bytes(got_b, n_b - 1, ar_send.at[1], ar_recv.at[1])
    got_c[me_a] = jnp.sum(got_b[...].astype(F32), axis=0).astype(BF16)

    for move in moves:
        pltpu.make_async_remote_copy(
            src_ref=got_c.at[me_a],
            dst_ref=got_c.at[me_a],
            send_sem=ar_send.at[2],
            recv_sem=ar_recv.at[2],
            device_id=plane_id(move)[1],
            device_id_type=MESH,
        ).start()

    parts[1].wait_recv()
    resid[pl.ds(0, 2)] = (acc[pl.ds(0, 2)] + left_in[pl.ds(0, 2)].astype(F32)).astype(BF16)
    solve(0)
    halos[2].wait_recv()
    halos[3].wait_recv()
    resid[6] = (acc[6] - upper_terms(6, [4])).astype(BF16)
    resid[7] = (acc[7] - upper_terms(7, [3, 4])).astype(BF16)
    solve(6)

    wait_bytes(got_c, n_a - 1, ar_send.at[2], ar_recv.at[2])
    zero_sum = got_c[pl.ds(0, n_a // 2)].reshape(TILE, TILE)
    one_sum = got_c[pl.ds(n_a // 2, n_a // 2)].reshape(TILE, TILE)
    mixed = dot(jnp.concatenate([one_sum, one_sum], axis=1), w_last[...])
    high, low = split(mixed[:, :TILE].T)
    cross_out[...] -= scale * dot(jnp.concatenate([high, high, low], axis=1), d_zero[...])
    mixed = mixed[:, TILE:]
    high, low = split(mixed + (mixed - zero_sum.astype(F32)).T)
    diag_out[...] += scale * dot_t(d_zero[...], jnp.concatenate([high, high, low], axis=0))

    for copy in halos + parts:
        copy.wait_send()


def body(band_tiles, band_mask, panels, panel_seed, diag_inverse, cross_block, cross_seed, diag_seed):
    n_col = lax.axis_size("col")
    plane_cols = min(PLANE_COLS, n_col // 2)
    n_a, n_b = 2 * plane_cols, n_col // plane_cols
    part = (WIDE // n_a, TILE)
    scale = 1.0 / math.sqrt(2 * n_col * ROWS * TILE)
    arrays = (band_tiles, band_mask, panels, panel_seed, diag_inverse, cross_block, cross_seed, diag_seed)
    any_spec = pl.BlockSpec(memory_space=pltpu.HBM)
    vmem = pl.BlockSpec(memory_space=pltpu.VMEM)
    dma = pltpu.SemaphoreType.DMA
    return tuple(
        pl.pallas_call(
            functools.partial(kernel, n_col, plane_cols, scale),
            out_shape=(
                pltpu.VMEM(panels.shape, BF16),
                pltpu.VMEM((TILE, TILE), F32),
                pltpu.VMEM((TILE, TILE), F32),
            ),
            in_specs=[any_spec] * 8,
            out_specs=(vmem, vmem, vmem),
            scratch_shapes=[
                pltpu.VMEM((ROWS, BAND + 1, TILE, TILE), BF16),
                pltpu.VMEM((ROWS + BAND, TILE, WIDE), BF16),
                pltpu.VMEM((ROWS, TILE, WIDE), BF16),
                pltpu.VMEM((ROWS, TILE, WIDE), F32),
                pltpu.VMEM((ROWS + BAND, TILE, WIDE), BF16),
                pltpu.VMEM((ROWS, TILE, TILE), BF16),
                pltpu.VMEM((BAND, TILE, WIDE), BF16),
                pltpu.VMEM((TILE, WIDE), F32),
                pltpu.VMEM((n_a,) + part, BF16),
                pltpu.VMEM((n_a,) + part, BF16),
                pltpu.VMEM((n_b,) + part, BF16),
                pltpu.VMEM((n_a,) + part, BF16),
                pltpu.VMEM(part, BF16),
                pltpu.VMEM((4 * TILE, TILE), BF16),
                pltpu.VMEM((2 * TILE, TILE), BF16),
                pltpu.VMEM((2 * TILE, WIDE), BF16),
                pltpu.VMEM((3 * TILE, TILE), BF16),
                pltpu.SMEM((ROWS, BAND + 1), jnp.int32),
                pltpu.VMEM((2, TILE, TILE), F32),
                pltpu.VMEM((TILE, TILE), BF16),
                pltpu.VMEM((TILE, TILE), F32),
                pltpu.VMEM((TILE, TILE), F32),
                dma((13,)),
                dma((2, 2)),
                dma((2, 2)),
                dma((2,)),
                dma((2,)),
                dma((3,)),
                dma((3,)),
            ],
            compiler_params=pltpu.CompilerParams(
                collective_id=0, has_side_effects=True, vmem_limit_bytes=40 * 1024 * 1024
            ),
        )(*(pltpu.with_memory_space_constraint(array, pltpu.HBM) for array in arrays))
    )


def solution(mesh):
    split_rows = P(("col", "row"), None, None, None)
    split_panels = P(None, ("col", "row"), None, None)
    return jax.shard_map(
        body,
        mesh=mesh,
        in_specs=(split_rows, P(("col", "row"), None), split_panels, split_panels, P(), P(), P(), P()),
        out_specs=(split_panels, P(), P()),
        check_vma=False,
    )
```

```python
import functools
import math

import jax
import jax.numpy as jnp
from jax import lax
from jax.experimental import pallas as pl
from jax.experimental.pallas import tpu as pltpu
from jax.sharding import PartitionSpec as P

MESH = pl.DeviceIdType.MESH
F32 = jnp.float32
BF16 = jnp.bfloat16
TILE = 256
WIDE = 512
ROWS = 8
BAND = 4
PLANE_COLS = 16


def dot(a, b):
    return jnp.dot(a, b, preferred_element_type=F32)


def dot_t(a, b):
    return lax.dot_general(a, b, (((0,), (0,)), ((), ())), preferred_element_type=F32)


def split(a):
    high = a.astype(BF16)
    return high, (a - high.astype(F32)).astype(BF16)


def dot_three(a, b):
    (a_high, a_low), (b_high, b_low) = split(a), split(b)
    return dot(jnp.concatenate([a_high, a_high, a_low], axis=1), jnp.concatenate([b_high, b_low, b_high], axis=0))


def kernel(
    n_col,
    plane_cols,
    band_hbm,
    mask_hbm,
    panels_hbm,
    seed_hbm,
    inverse_hbm,
    cross_hbm,
    cross_seed_hbm,
    diag_seed_hbm,
    out_v,
    sums,
    w_last,
    d_zero,
    cross_base,
    diag_base,
    tiles,
    rows,
    seeds,
    acc,
    resid,
    negm,
    left_in,
    total,
    staged,
    got_a,
    got_b,
    got_c,
    mine,
    w_zero,
    w_one,
    mask,
    diag_inverse,
    cross_block,
    cross_seed,
    diag_seed,
    in_sem,
    halo_send,
    halo_recv,
    part_send,
    part_recv,
    ar_send,
    ar_recv,
):
    col, row = lax.axis_index("col"), lax.axis_index("row")
    n_dev = 2 * n_col
    index = col * 2 + row
    left, right = lax.rem(index + n_dev - 1, n_dev), lax.rem(index + 1, n_dev)
    left_id = (left // 2, lax.rem(left, 2))
    right_id = (right // 2, lax.rem(right, 2))
    n_a = 2 * plane_cols
    n_b = n_col // plane_cols
    depth, place = col // plane_cols, lax.rem(col, plane_cols)
    me_a = place * 2 + row

    side = math.isqrt(plane_cols) if math.isqrt(plane_cols) ** 2 == plane_cols else 1
    width = plane_cols // side
    moves = [(dx, dy, dc) for dx in range(side) for dy in range(width) for dc in range(2)][1:]
    moves.sort(key=lambda m: -min(m[0], side - m[0]) - min(m[1], width - m[1]))

    def plane_id(move):
        dx, dy, dc = move
        peer_x = lax.rem(place // width + dx, side)
        peer_place = peer_x * width + lax.rem(lax.rem(place, width) + dy, width)
        peer_row = lax.rem(row + dc, 2)
        return peer_place * 2 + peer_row, (depth * plane_cols + peer_place, peer_row)

    line_steps = sorted(range(1, n_b), key=lambda k: -min(k, n_b - k))

    def line_id(step):
        return (lax.rem(depth + step, n_b) * plane_cols + place, row)

    barrier = pltpu.get_barrier_semaphore()
    pl.semaphore_signal(barrier, inc=1, device_id=left_id, device_id_type=MESH)
    pl.semaphore_signal(barrier, inc=1, device_id=right_id, device_id_type=MESH)

    def load(source, target, slot):
        copy = pltpu.make_async_copy(source, target, in_sem.at[slot])
        copy.start()
        return copy

    upper, lower = pl.ds(4, 4), pl.ds(0, 4)
    first, second = pl.ds(0, TILE), pl.ds(TILE, TILE)
    loads_hi = [
        load(mask_hbm, mask, 8),
        load(panels_hbm.at[0, upper], rows.at[upper, :, first], 0),
        load(panels_hbm.at[1, upper], rows.at[upper, :, second], 1),
        load(band_hbm.at[upper], tiles.at[upper], 2),
    ]

    for step in range(1, n_b):
        pl.semaphore_signal(barrier, inc=1, device_id=line_id(step), device_id_type=MESH)
    for move in moves:
        pl.semaphore_signal(barrier, inc=1, device_id=plane_id(move)[1], device_id_type=MESH)

    loads_lo = [
        load(panels_hbm.at[0, lower], rows.at[lower, :, first], 3),
        load(panels_hbm.at[1, lower], rows.at[lower, :, second], 4),
        load(band_hbm.at[lower], tiles.at[lower], 5),
        load(seed_hbm.at[0], seeds.at[:, :, first], 6),
        load(seed_hbm.at[1], seeds.at[:, :, second], 7),
    ]
    loads_last = [
        load(inverse_hbm, diag_inverse, 9),
        load(cross_hbm, cross_block, 10),
        load(cross_seed_hbm, cross_seed, 11),
        load(diag_seed_hbm, diag_seed, 12),
    ]

    def tile(c, d):
        keep = jnp.full((TILE, TILE), mask[c, d].astype(F32), F32).astype(BF16)
        return tiles[c, d] * keep

    def lower_terms(r, slots):
        lhs = jnp.concatenate([tile(r - d, d) for d in slots], axis=1)
        rhs = rows[pl.ds(r - slots[0], len(slots))].reshape(len(slots) * TILE, WIDE)
        return dot(lhs, rhs)

    def upper_terms(i, slots):
        lhs = jnp.concatenate([tile(i, d) for d in slots], axis=0)
        rhs = rows[pl.ds(i + slots[0], len(slots))].reshape(len(slots) * TILE, WIDE)
        return dot_t(lhs, rhs)

    halos = []
    for begin in (0, 2):
        for p, lanes in ((0, first), (1, second)):
            halos.append(
                pltpu.make_async_remote_copy(
                    src_ref=panels_hbm.at[p, pl.ds(begin, 2)],
                    dst_ref=rows.at[pl.ds(8 + begin, 2), :, lanes],
                    send_sem=halo_send.at[p, begin // 2],
                    recv_sem=halo_recv.at[p, begin // 2],
                    device_id=left_id,
                    device_id_type=MESH,
                )
            )
    parts = []
    for begin in (2, 0):
        for p, lanes in ((0, first), (1, second)):
            parts.append(
                pltpu.make_async_remote_copy(
                    src_ref=resid.at[pl.ds(8 + begin, 2), :, lanes],
                    dst_ref=left_in.at[pl.ds(begin, 2), :, lanes],
                    send_sem=part_send.at[p, begin // 2],
                    recv_sem=part_recv.at[p, begin // 2],
                    device_id=right_id,
                    device_id_type=MESH,
                )
            )

    pl.semaphore_wait(barrier, n_a + n_b)
    halos[0].start()
    halos[1].start()

    for copy in loads_hi:
        copy.wait()
    for r in (11, 10):
        resid[r] = (-lower_terms(r, list(range(4, r - 8, -1)))).astype(BF16)
    parts[0].start()
    parts[1].start()
    for r in (9, 8):
        resid[r] = (-lower_terms(r, list(range(4, r - 8, -1)))).astype(BF16)

    def own_terms(i, slots):
        value = seeds[i].astype(F32)
        turned = -dot(tile(i, 0), rows[i, :, :TILE])
        if slots:
            terms = lower_terms(i, slots)
            value = value - terms
            turned = turned - terms[:, :TILE]
        acc[i] = value
        resid[i] = value.astype(BF16)
        negm[i] = turned.astype(BF16)

    def sum_over(i):
        lhs = jnp.concatenate([rows[i, :, :TILE], negm[i]], axis=0)
        rhs = jnp.concatenate([resid[i], rows[i]], axis=0)
        return dot_t(lhs, rhs)

    for copy in loads_lo:
        copy.wait()
    total[...] = jnp.zeros_like(total)

    @pl.loop(4, 8)
    def _(i):
        own_terms(i, [4, 3, 2, 1])
        total[...] += sum_over(i)

    for i in range(4):
        own_terms(i, list(range(i, 0, -1)))

    @pl.loop(0, 2)
    def _(i):
        total[...] += sum_over(i)

    edge = (2, 3)
    beyond = (8, 9)
    part_rows = 2 * TILE // n_a
    half = n_a // 2

    def wait_bytes(buffer, count, stage, p):
        view = buffer.at[p, pl.ds(0, count)]
        pltpu.make_async_copy(view, view, ar_recv.at[stage, p]).wait()
        pltpu.make_async_copy(view, view, ar_send.at[stage, p]).wait()

    def scatter(p):
        for move in moves:
            peer, peer_id = plane_id(move)
            pltpu.make_async_remote_copy(
                src_ref=staged.at[p, peer],
                dst_ref=got_a.at[p, me_a],
                send_sem=ar_send.at[0, p],
                recv_sem=ar_recv.at[0, p],
                device_id=peer_id,
                device_id_type=MESH,
            ).start()
        got_a[p, me_a] = staged[p, me_a]

    def across(p):
        wait_bytes(got_a, n_a - 1, 0, p)
        mine[p] = jnp.sum(got_a[p].astype(F32), axis=0).astype(BF16)
        for step in line_steps:
            pltpu.make_async_remote_copy(
                src_ref=mine.at[p],
                dst_ref=got_b.at[p, depth],
                send_sem=ar_send.at[1, p],
                recv_sem=ar_recv.at[1, p],
                device_id=line_id(step),
                device_id_type=MESH,
            ).start()
        got_b[p, depth] = mine[p]

    def gather(p):
        wait_bytes(got_b, n_b - 1, 1, p)
        got_c[p, me_a] = jnp.sum(got_b[p].astype(F32), axis=0).astype(BF16)
        for move in moves:
            pltpu.make_async_remote_copy(
                src_ref=got_c.at[p, me_a],
                dst_ref=got_c.at[p, me_a],
                send_sem=ar_send.at[2, p],
                recv_sem=ar_recv.at[2, p],
                device_id=plane_id(move)[1],
                device_id_type=MESH,
            ).start()

    for p in range(2):
        begin = p * TILE
        parts[p].wait_recv()
        for i in edge:
            arrived = left_in[i, :, begin : begin + TILE].astype(F32)
            value = acc[i, :, begin : begin + TILE] + arrived
            acc[i, :, begin : begin + TILE] = value
            resid[i, :, begin : begin + TILE] = value.astype(BF16)
            if p == 0:
                negm[i] = (negm[i].astype(F32) + arrived).astype(BF16)
        halos[p].wait_recv()
        lhs = [rows[i, :, :TILE] for i in edge + beyond] + [negm[i] for i in edge]
        lhs += [resid[i, :, :TILE] for i in beyond]
        rhs = [resid[i, :, begin : begin + TILE] for i in edge + beyond]
        rhs += [rows[i, :, begin : begin + TILE] for i in edge + beyond]
        value = total[:, begin : begin + TILE]
        value = value + dot_t(jnp.concatenate(lhs, axis=0), jnp.concatenate(rhs, axis=0))
        value = value.astype(BF16)
        for k in range(2):
            staged[p, pl.ds(k * half, half)] = value[:, k * 128 : (k + 1) * 128].reshape(half, part_rows, 128)
        scatter(p)

    for copy in halos[2:] + parts[2:]:
        copy.start()
    for copy in loads_last:
        copy.wait()

    zero_high, zero_low = split(diag_inverse[0])
    one_high, one_low = split(diag_inverse[1])
    cross = cross_block[...]
    crosses = jnp.concatenate([cross, cross], axis=0)
    through = dot(jnp.concatenate([one_high, one_low], axis=1), crosses)
    through_high, through_low = split(through)
    carry_high, carry_low = split(-dot_three(through, diag_inverse[0]))
    w_zero[...] = jnp.concatenate([zero_high, carry_high, zero_low, carry_low], axis=0)
    w_one[...] = jnp.concatenate([one_high, one_low], axis=0)
    w_last[:TILE] = jnp.concatenate([one_high, through_high], axis=1)
    w_last[TILE:] = jnp.concatenate([one_low, through_low], axis=1)
    d_zero[...] = jnp.concatenate([zero_high, zero_low, zero_high], axis=0)
    base = dot_three(cross_seed[...], diag_inverse[0])
    cross_base[...] = base
    diag_base[...] = diag_seed[...] - dot_t(jnp.concatenate(split(base), axis=0), crosses)

    @pl.loop(0, 4)
    def _(i):
        acc[i] = acc[i] - upper_terms(i, [0, 1, 2, 3, 4])

    def solve(begin):
        value = resid[pl.ds(begin, 2)].reshape(2 * TILE, WIDE)
        one = value[:, TILE:]
        zero_term = dot(jnp.concatenate([value, value], axis=1), w_zero[...])
        one_term = dot(jnp.concatenate([one, one], axis=1), w_one[...])
        for p, term in ((0, zero_term), (1, one_term)):
            out_v[p, pl.ds(begin, 2)] = term.astype(BF16).reshape(2, TILE, TILE)

    across(0)

    resid[pl.ds(2, 2)] = acc[pl.ds(2, 2)].astype(BF16)
    solve(2)
    across(1)

    @pl.loop(4, 6)
    def _(i):
        resid[i] = (acc[i] - upper_terms(i, [0, 1, 2, 3, 4])).astype(BF16)

    acc[6] = acc[6] - upper_terms(6, [0, 1, 2, 3])
    acc[7] = acc[7] - upper_terms(7, [0, 1, 2])
    gather(0)

    solve(4)
    gather(1)

    for copy in parts[2:] + halos[2:]:
        copy.wait_recv()
    resid[pl.ds(0, 2)] = (acc[pl.ds(0, 2)] + left_in[pl.ds(0, 2)].astype(F32)).astype(BF16)
    solve(0)
    resid[6] = (acc[6] - upper_terms(6, [4])).astype(BF16)
    resid[7] = (acc[7] - upper_terms(7, [3, 4])).astype(BF16)
    solve(6)
    for copy in halos + parts:
        copy.wait_send()

    for p in range(2):
        wait_bytes(got_c, n_a - 1, 2, p)
        for k in range(2):
            sums[p, :, k * 128 : (k + 1) * 128] = got_c[p, pl.ds(k * half, half)].reshape(TILE, 128)


def finish(
    scale,
    out_v,
    sums,
    w_last,
    d_zero,
    cross_base,
    diag_base,
    out_hbm,
    cross_hbm,
    diag_hbm,
    cross_v,
    diag_v,
    sem,
):
    copies = [
        pltpu.make_async_copy(out_v, out_hbm, sem.at[0]),
        pltpu.make_async_copy(cross_v, cross_hbm, sem.at[1]),
        pltpu.make_async_copy(diag_v, diag_hbm, sem.at[2]),
    ]
    copies[0].start()
    one_sum = sums[1]
    mixed = dot(jnp.concatenate([one_sum, one_sum], axis=1), w_last[...])
    high, low = split(mixed[:, :TILE].T)
    cross_v[...] = cross_base[...] - scale * dot(jnp.concatenate([high, high, low], axis=1), d_zero[...])
    copies[1].start()
    mixed = mixed[:, TILE:]
    high, low = split(mixed + (mixed - sums[0].astype(F32)).T)
    diag_v[...] = diag_base[...] + scale * dot_t(d_zero[...], jnp.concatenate([high, high, low], axis=0))
    copies[2].start()
    for copy in copies:
        copy.wait()


def body(band_tiles, band_mask, panels, panel_seed, diag_inverse, cross_block, cross_seed, diag_seed):
    n_col = lax.axis_size("col")
    plane_cols = min(PLANE_COLS, n_col // 2)
    n_a, n_b = 2 * plane_cols, n_col // plane_cols
    part = (2 * TILE // n_a, 128)
    scale = 1.0 / math.sqrt(2 * n_col * ROWS * TILE)
    arrays = (band_tiles, band_mask, panels, panel_seed, diag_inverse, cross_block, cross_seed, diag_seed)
    any_spec = pl.BlockSpec(memory_space=pltpu.HBM)
    vmem = pl.BlockSpec(memory_space=pltpu.VMEM)
    dma = pltpu.SemaphoreType.DMA
    held = pl.pallas_call(
        functools.partial(kernel, n_col, plane_cols),
        out_shape=(
            pltpu.VMEM(panels.shape, BF16),
            pltpu.VMEM((2, TILE, TILE), BF16),
            pltpu.VMEM((2 * TILE, WIDE), BF16),
            pltpu.VMEM((3 * TILE, TILE), BF16),
            pltpu.VMEM((TILE, TILE), F32),
            pltpu.VMEM((TILE, TILE), F32),
        ),
        in_specs=[any_spec] * 8,
        out_specs=(vmem,) * 6,
        scratch_shapes=[
            pltpu.VMEM((ROWS, BAND + 1, TILE, TILE), BF16),
            pltpu.VMEM((ROWS + BAND, TILE, WIDE), BF16),
            pltpu.VMEM((ROWS, TILE, WIDE), BF16),
            pltpu.VMEM((ROWS, TILE, WIDE), F32),
            pltpu.VMEM((ROWS + BAND, TILE, WIDE), BF16),
            pltpu.VMEM((ROWS, TILE, TILE), BF16),
            pltpu.VMEM((BAND, TILE, WIDE), BF16),
            pltpu.VMEM((TILE, WIDE), F32),
            pltpu.VMEM((2, n_a) + part, BF16),
            pltpu.VMEM((2, n_a) + part, BF16),
            pltpu.VMEM((2, n_b) + part, BF16),
            pltpu.VMEM((2, n_a) + part, BF16),
            pltpu.VMEM((2,) + part, BF16),
            pltpu.VMEM((4 * TILE, TILE), BF16),
            pltpu.VMEM((2 * TILE, TILE), BF16),
            pltpu.SMEM((ROWS, BAND + 1), jnp.int32),
            pltpu.VMEM((2, TILE, TILE), F32),
            pltpu.VMEM((TILE, TILE), BF16),
            pltpu.VMEM((TILE, TILE), F32),
            pltpu.VMEM((TILE, TILE), F32),
            dma((13,)),
            dma((2, 2)),
            dma((2, 2)),
            dma((2, 2)),
            dma((2, 2)),
            dma((3, 2)),
            dma((3, 2)),
        ],
        compiler_params=pltpu.CompilerParams(
            collective_id=0, has_side_effects=True, vmem_limit_bytes=40 * 1024 * 1024
        ),
    )(*(pltpu.with_memory_space_constraint(array, pltpu.HBM) for array in arrays))
    return tuple(
        pl.pallas_call(
            functools.partial(finish, scale),
            out_shape=(
                jax.ShapeDtypeStruct(panels.shape, BF16),
                jax.ShapeDtypeStruct((TILE, TILE), F32),
                jax.ShapeDtypeStruct((TILE, TILE), F32),
            ),
            in_specs=[vmem] * 6,
            out_specs=(pl.BlockSpec(memory_space=pl.ANY),) * 3,
            scratch_shapes=[
                pltpu.VMEM((TILE, TILE), F32),
                pltpu.VMEM((TILE, TILE), F32),
                dma((3,)),
            ],
            compiler_params=pltpu.CompilerParams(vmem_limit_bytes=16 * 1024 * 1024),
        )(*(pltpu.with_memory_space_constraint(array, pltpu.VMEM) for array in held))
    )


def solution(mesh):
    split_rows = P(("col", "row"), None, None, None)
    split_panels = P(None, ("col", "row"), None, None)
    return jax.shard_map(
        body,
        mesh=mesh,
        in_specs=(split_rows, P(("col", "row"), None), split_panels, split_panels, P(), P(), P(), P()),
        out_specs=(split_panels, P(), P()),
        check_vma=False,
    )
```

```python
import functools
import math

import jax
import jax.numpy as jnp
from jax import lax
from jax.experimental import pallas as pl
from jax.experimental.pallas import tpu as pltpu
from jax.sharding import PartitionSpec as P

MESH = pl.DeviceIdType.MESH
F32 = jnp.float32
BF16 = jnp.bfloat16
TILE = 256
WIDE = 512
ROWS = 8
BAND = 4
PLANE_COLS = 16


def dot(a, b):
    return jnp.dot(a, b, preferred_element_type=F32)


def dot_t(a, b):
    return lax.dot_general(a, b, (((0,), (0,)), ((), ())), preferred_element_type=F32)


def split(a):
    high = a.astype(BF16)
    return high, (a - high.astype(F32)).astype(BF16)


def dot_three(a, b):
    (a_high, a_low), (b_high, b_low) = split(a), split(b)
    return dot(jnp.concatenate([a_high, a_high, a_low], axis=1), jnp.concatenate([b_high, b_low, b_high], axis=0))


def kernel(
    n_col,
    plane_cols,
    band_hbm,
    mask_hbm,
    panels_hbm,
    seed_hbm,
    inverse_hbm,
    cross_hbm,
    cross_seed_hbm,
    diag_seed_hbm,
    out_v,
    sums,
    w_last,
    d_zero,
    cross_base,
    diag_base,
    tiles,
    rows,
    seeds,
    acc,
    resid,
    negm,
    left_in,
    total,
    staged,
    got_a,
    got_b,
    got_c,
    mine,
    w_zero,
    w_one,
    mask,
    diag_inverse,
    cross_block,
    cross_seed,
    diag_seed,
    in_sem,
    halo_send,
    halo_recv,
    part_send,
    part_recv,
    ar_send,
    ar_recv,
):
    col, row = lax.axis_index("col"), lax.axis_index("row")
    n_dev = 2 * n_col
    index = col * 2 + row
    left, right = lax.rem(index + n_dev - 1, n_dev), lax.rem(index + 1, n_dev)
    left_id = (left // 2, lax.rem(left, 2))
    right_id = (right // 2, lax.rem(right, 2))
    n_a = 2 * plane_cols
    n_b = n_col // plane_cols
    depth, place = col // plane_cols, lax.rem(col, plane_cols)
    me_a = place * 2 + row

    side = math.isqrt(plane_cols) if math.isqrt(plane_cols) ** 2 == plane_cols else 1
    width = plane_cols // side
    moves = [(dx, dy, dc) for dx in range(side) for dy in range(width) for dc in range(2)][1:]
    moves.sort(key=lambda m: -min(m[0], side - m[0]) - min(m[1], width - m[1]))

    def plane_id(move):
        dx, dy, dc = move
        peer_x = lax.rem(place // width + dx, side)
        peer_place = peer_x * width + lax.rem(lax.rem(place, width) + dy, width)
        peer_row = lax.rem(row + dc, 2)
        return peer_place * 2 + peer_row, (depth * plane_cols + peer_place, peer_row)

    line_steps = sorted(range(1, n_b), key=lambda k: -min(k, n_b - k))

    def line_id(step):
        return (lax.rem(depth + step, n_b) * plane_cols + place, row)

    barrier = pltpu.get_barrier_semaphore()
    pl.semaphore_signal(barrier, inc=1, device_id=left_id, device_id_type=MESH)
    pl.semaphore_signal(barrier, inc=1, device_id=right_id, device_id_type=MESH)

    def load(source, target, slot):
        copy = pltpu.make_async_copy(source, target, in_sem.at[slot])
        copy.start()
        return copy

    lower, edge_rows, middle = pl.ds(0, 4), pl.ds(6, 2), pl.ds(4, 2)
    first, second = pl.ds(0, TILE), pl.ds(TILE, TILE)
    loads_edge = [
        load(mask_hbm, mask, 0),
        load(band_hbm.at[edge_rows], tiles.at[edge_rows], 1),
        load(panels_hbm.at[0, edge_rows], rows.at[edge_rows, :, first], 2),
        load(panels_hbm.at[1, edge_rows], rows.at[edge_rows, :, second], 3),
    ]

    for step in line_steps:
        pl.semaphore_signal(barrier, inc=1, device_id=line_id(step), device_id_type=MESH)
    for move in moves:
        pl.semaphore_signal(barrier, inc=1, device_id=plane_id(move)[1], device_id_type=MESH)

    loads_hi = [
        load(band_hbm.at[middle], tiles.at[middle], 4),
        load(panels_hbm.at[0, middle], rows.at[middle, :, first], 5),
        load(panels_hbm.at[1, middle], rows.at[middle, :, second], 6),
    ]
    loads_lo = [
        load(panels_hbm.at[0, lower], rows.at[lower, :, first], 7),
        load(panels_hbm.at[1, lower], rows.at[lower, :, second], 8),
        load(band_hbm.at[lower], tiles.at[lower], 9),
        load(seed_hbm.at[0], seeds.at[:, :, first], 10),
        load(seed_hbm.at[1], seeds.at[:, :, second], 11),
    ]
    loads_last = [
        load(inverse_hbm, diag_inverse, 12),
        load(cross_hbm, cross_block, 13),
        load(cross_seed_hbm, cross_seed, 14),
        load(diag_seed_hbm, diag_seed, 15),
    ]

    def tile(c, d):
        keep = jnp.full((TILE, TILE), mask[c, d].astype(F32), F32).astype(BF16)
        return tiles[c, d] * keep

    def lower_terms(r, slots):
        lhs = jnp.concatenate([tile(r - d, d) for d in slots], axis=1)
        rhs = rows[pl.ds(r - slots[0], len(slots))].reshape(len(slots) * TILE, WIDE)
        return dot(lhs, rhs)

    def upper_terms(i, slots):
        lhs = jnp.concatenate([tile(i, d) for d in slots], axis=0)
        rhs = rows[pl.ds(i + slots[0], len(slots))].reshape(len(slots) * TILE, WIDE)
        return dot_t(lhs, rhs)

    halos = []
    for begin in (0, 2):
        for p, lanes in ((0, first), (1, second)):
            halos.append(
                pltpu.make_async_remote_copy(
                    src_ref=panels_hbm.at[p, pl.ds(begin, 2)],
                    dst_ref=rows.at[pl.ds(8 + begin, 2), :, lanes],
                    send_sem=halo_send.at[p, begin // 2],
                    recv_sem=halo_recv.at[p, begin // 2],
                    device_id=left_id,
                    device_id_type=MESH,
                )
            )
    parts = []
    for begin in (2, 0):
        for p, lanes in ((0, first), (1, second)):
            parts.append(
                pltpu.make_async_remote_copy(
                    src_ref=resid.at[pl.ds(8 + begin, 2), :, lanes],
                    dst_ref=left_in.at[pl.ds(begin, 2), :, lanes],
                    send_sem=part_send.at[p, begin // 2],
                    recv_sem=part_recv.at[p, begin // 2],
                    device_id=right_id,
                    device_id_type=MESH,
                )
            )

    for copy in loads_edge:
        copy.wait()
    for r in (11, 10):
        resid[r] = (-lower_terms(r, list(range(4, r - 8, -1)))).astype(BF16)

    pl.semaphore_wait(barrier, n_a + n_b)
    halos[0].start()
    halos[1].start()
    parts[0].start()
    parts[1].start()
    for copy in loads_hi:
        copy.wait()
    for r in (9, 8):
        resid[r] = (-lower_terms(r, list(range(4, r - 8, -1)))).astype(BF16)

    def own_terms(i, slots):
        value = seeds[i].astype(F32)
        turned = -dot(tile(i, 0), rows[i, :, :TILE])
        if slots:
            terms = lower_terms(i, slots)
            value = value - terms
            turned = turned - terms[:, :TILE]
        acc[i] = value
        resid[i] = value.astype(BF16)
        negm[i] = turned.astype(BF16)

    def sum_over(i):
        lhs = jnp.concatenate([rows[i, :, :TILE], negm[i]], axis=0)
        rhs = jnp.concatenate([resid[i], rows[i]], axis=0)
        return dot_t(lhs, rhs)

    for copy in loads_lo:
        copy.wait()
    total[...] = jnp.zeros_like(total)

    @pl.loop(4, 8)
    def _(i):
        own_terms(i, [4, 3, 2, 1])
        total[...] += sum_over(i)

    for i in range(4):
        own_terms(i, list(range(i, 0, -1)))

    @pl.loop(0, 2)
    def _(i):
        total[...] += sum_over(i)

    edge = (2, 3)
    beyond = (8, 9)
    part_rows = 2 * TILE // n_a
    half = n_a // 2

    def wait_bytes(buffer, count, stage, p):
        view = buffer.at[p, pl.ds(0, count)]
        pltpu.make_async_copy(view, view, ar_recv.at[stage, p]).wait()
        pltpu.make_async_copy(view, view, ar_send.at[stage, p]).wait()

    def scatter(p):
        for move in moves:
            peer, peer_id = plane_id(move)
            pltpu.make_async_remote_copy(
                src_ref=staged.at[p, peer],
                dst_ref=got_a.at[p, me_a],
                send_sem=ar_send.at[0, p],
                recv_sem=ar_recv.at[0, p],
                device_id=peer_id,
                device_id_type=MESH,
            ).start()
        got_a[p, me_a] = staged[p, me_a]

    def across(p):
        wait_bytes(got_a, n_a - 1, 0, p)
        mine[p] = jnp.sum(got_a[p].astype(F32), axis=0).astype(BF16)
        for step in line_steps:
            pltpu.make_async_remote_copy(
                src_ref=mine.at[p],
                dst_ref=got_b.at[p, depth],
                send_sem=ar_send.at[1, p],
                recv_sem=ar_recv.at[1, p],
                device_id=line_id(step),
                device_id_type=MESH,
            ).start()
        got_b[p, depth] = mine[p]

    def gather(p):
        wait_bytes(got_b, n_b - 1, 1, p)
        got_c[p, me_a] = jnp.sum(got_b[p].astype(F32), axis=0).astype(BF16)
        for move in moves:
            pltpu.make_async_remote_copy(
                src_ref=got_c.at[p, me_a],
                dst_ref=got_c.at[p, me_a],
                send_sem=ar_send.at[2, p],
                recv_sem=ar_recv.at[2, p],
                device_id=plane_id(move)[1],
                device_id_type=MESH,
            ).start()

    for p in range(2):
        begin = p * TILE
        if p == 1:
            lhs = [negm[i] for i in edge] + [rows[i, :, :TILE] for i in beyond]
            rhs = [rows[i, :, begin : begin + TILE] for i in edge]
            rhs += [resid[i, :, begin : begin + TILE] for i in beyond]
            total[:, begin : begin + TILE] += dot_t(jnp.concatenate(lhs, axis=0), jnp.concatenate(rhs, axis=0))
        parts[p].wait_recv()
        for i in edge:
            arrived = left_in[i, :, begin : begin + TILE].astype(F32)
            value = acc[i, :, begin : begin + TILE] + arrived
            acc[i, :, begin : begin + TILE] = value
            resid[i, :, begin : begin + TILE] = value.astype(BF16)
            if p == 0:
                negm[i] = (negm[i].astype(F32) + arrived).astype(BF16)
        halos[p].wait_recv()
        lhs = [rows[i, :, :TILE] for i in edge] + [resid[i, :, :TILE] for i in beyond]
        rhs = [resid[i, :, begin : begin + TILE] for i in edge]
        rhs += [rows[i, :, begin : begin + TILE] for i in beyond]
        if p == 0:
            lhs += [negm[i] for i in edge] + [rows[i, :, :TILE] for i in beyond]
            rhs += [rows[i, :, begin : begin + TILE] for i in edge]
            rhs += [resid[i, :, begin : begin + TILE] for i in beyond]
        value = total[:, begin : begin + TILE]
        value = value + dot_t(jnp.concatenate(lhs, axis=0), jnp.concatenate(rhs, axis=0))
        value = value.astype(BF16)
        for k in range(2):
            staged[p, pl.ds(k * half, half)] = value[:, k * 128 : (k + 1) * 128].reshape(half, part_rows, 128)
        scatter(p)

    for copy in (halos[2], parts[2]):
        copy.start()
    for copy in loads_last:
        copy.wait()

    zero_high, zero_low = split(diag_inverse[0])
    one_high, one_low = split(diag_inverse[1])
    cross = cross_block[...]
    crosses = jnp.concatenate([cross, cross], axis=0)
    through = dot(jnp.concatenate([one_high, one_low], axis=1), crosses)
    through_high, through_low = split(through)
    carry_high, carry_low = split(-dot_three(through, diag_inverse[0]))
    w_zero[...] = jnp.concatenate([zero_high, carry_high, zero_low, carry_low], axis=0)
    w_one[...] = jnp.concatenate([one_high, one_low], axis=0)
    w_last[:TILE] = jnp.concatenate([one_high, through_high], axis=1)
    w_last[TILE:] = jnp.concatenate([one_low, through_low], axis=1)
    d_zero[...] = jnp.concatenate([zero_high, zero_low, zero_high], axis=0)
    base = dot_three(cross_seed[...], diag_inverse[0])
    cross_base[...] = base
    diag_base[...] = diag_seed[...] - dot_t(jnp.concatenate(split(base), axis=0), crosses)

    @pl.loop(0, 4)
    def _(i):
        acc[i] = acc[i] - upper_terms(i, [0, 1, 2, 3, 4])

    def solve(begin):
        value = resid[pl.ds(begin, 2)].reshape(2 * TILE, WIDE)
        one = value[:, TILE:]
        zero_term = dot(jnp.concatenate([value, value], axis=1), w_zero[...])
        one_term = dot(jnp.concatenate([one, one], axis=1), w_one[...])
        for p, term in ((0, zero_term), (1, one_term)):
            out_v[p, pl.ds(begin, 2)] = term.astype(BF16).reshape(2, TILE, TILE)

    across(0)

    resid[pl.ds(2, 2)] = acc[pl.ds(2, 2)].astype(BF16)
    solve(2)
    for copy in (halos[3], parts[3]):
        copy.start()
    across(1)

    @pl.loop(4, 6)
    def _(i):
        resid[i] = (acc[i] - upper_terms(i, [0, 1, 2, 3, 4])).astype(BF16)

    acc[6] = acc[6] - upper_terms(6, [0, 1, 2, 3])
    acc[7] = acc[7] - upper_terms(7, [0, 1, 2])
    gather(0)

    solve(4)
    gather(1)

    for copy in parts[2:] + halos[2:]:
        copy.wait_recv()
    resid[pl.ds(0, 2)] = (acc[pl.ds(0, 2)] + left_in[pl.ds(0, 2)].astype(F32)).astype(BF16)
    solve(0)
    resid[6] = (acc[6] - upper_terms(6, [4])).astype(BF16)
    resid[7] = (acc[7] - upper_terms(7, [3, 4])).astype(BF16)
    solve(6)
    for copy in halos + parts:
        copy.wait_send()

    for p in range(2):
        wait_bytes(got_c, n_a - 1, 2, p)
        for k in range(2):
            sums[p, :, k * 128 : (k + 1) * 128] = got_c[p, pl.ds(k * half, half)].reshape(TILE, 128)


def finish(
    scale,
    out_v,
    sums,
    w_last,
    d_zero,
    cross_base,
    diag_base,
    out_hbm,
    cross_hbm,
    diag_hbm,
    cross_v,
    diag_v,
    sem,
):
    copies = [
        pltpu.make_async_copy(out_v, out_hbm, sem.at[0]),
        pltpu.make_async_copy(cross_v, cross_hbm, sem.at[1]),
        pltpu.make_async_copy(diag_v, diag_hbm, sem.at[2]),
    ]
    copies[0].start()
    one_sum = sums[1]
    mixed = dot(jnp.concatenate([one_sum, one_sum], axis=1), w_last[...])
    high, low = split(mixed[:, :TILE].T)
    cross_v[...] = cross_base[...] - scale * dot(jnp.concatenate([high, high, low], axis=1), d_zero[...])
    copies[1].start()
    mixed = mixed[:, TILE:]
    high, low = split(mixed + (mixed - sums[0].astype(F32)).T)
    diag_v[...] = diag_base[...] + scale * dot_t(d_zero[...], jnp.concatenate([high, high, low], axis=0))
    copies[2].start()
    for copy in copies:
        copy.wait()


def body(band_tiles, band_mask, panels, panel_seed, diag_inverse, cross_block, cross_seed, diag_seed):
    n_col = lax.axis_size("col")
    plane_cols = min(PLANE_COLS, n_col // 2)
    n_a, n_b = 2 * plane_cols, n_col // plane_cols
    part = (2 * TILE // n_a, 128)
    scale = 1.0 / math.sqrt(2 * n_col * ROWS * TILE)
    arrays = (band_tiles, band_mask, panels, panel_seed, diag_inverse, cross_block, cross_seed, diag_seed)
    any_spec = pl.BlockSpec(memory_space=pltpu.HBM)
    vmem = pl.BlockSpec(memory_space=pltpu.VMEM)
    dma = pltpu.SemaphoreType.DMA
    held = pl.pallas_call(
        functools.partial(kernel, n_col, plane_cols),
        out_shape=(
            pltpu.VMEM(panels.shape, BF16),
            pltpu.VMEM((2, TILE, TILE), BF16),
            pltpu.VMEM((2 * TILE, WIDE), BF16),
            pltpu.VMEM((3 * TILE, TILE), BF16),
            pltpu.VMEM((TILE, TILE), F32),
            pltpu.VMEM((TILE, TILE), F32),
        ),
        in_specs=[any_spec] * 8,
        out_specs=(vmem,) * 6,
        scratch_shapes=[
            pltpu.VMEM((ROWS, BAND + 1, TILE, TILE), BF16),
            pltpu.VMEM((ROWS + BAND, TILE, WIDE), BF16),
            pltpu.VMEM((ROWS, TILE, WIDE), BF16),
            pltpu.VMEM((ROWS, TILE, WIDE), F32),
            pltpu.VMEM((ROWS + BAND, TILE, WIDE), BF16),
            pltpu.VMEM((ROWS, TILE, TILE), BF16),
            pltpu.VMEM((BAND, TILE, WIDE), BF16),
            pltpu.VMEM((TILE, WIDE), F32),
            pltpu.VMEM((2, n_a) + part, BF16),
            pltpu.VMEM((2, n_a) + part, BF16),
            pltpu.VMEM((2, n_b) + part, BF16),
            pltpu.VMEM((2, n_a) + part, BF16),
            pltpu.VMEM((2,) + part, BF16),
            pltpu.VMEM((4 * TILE, TILE), BF16),
            pltpu.VMEM((2 * TILE, TILE), BF16),
            pltpu.SMEM((ROWS, BAND + 1), jnp.int32),
            pltpu.VMEM((2, TILE, TILE), F32),
            pltpu.VMEM((TILE, TILE), BF16),
            pltpu.VMEM((TILE, TILE), F32),
            pltpu.VMEM((TILE, TILE), F32),
            dma((16,)),
            dma((2, 2)),
            dma((2, 2)),
            dma((2, 2)),
            dma((2, 2)),
            dma((3, 2)),
            dma((3, 2)),
        ],
        compiler_params=pltpu.CompilerParams(
            collective_id=0, has_side_effects=True, vmem_limit_bytes=40 * 1024 * 1024
        ),
    )(*(pltpu.with_memory_space_constraint(array, pltpu.HBM) for array in arrays))
    return tuple(
        pl.pallas_call(
            functools.partial(finish, scale),
            out_shape=(
                jax.ShapeDtypeStruct(panels.shape, BF16),
                jax.ShapeDtypeStruct((TILE, TILE), F32),
                jax.ShapeDtypeStruct((TILE, TILE), F32),
            ),
            in_specs=[vmem] * 6,
            out_specs=(pl.BlockSpec(memory_space=pl.ANY),) * 3,
            scratch_shapes=[
                pltpu.VMEM((TILE, TILE), F32),
                pltpu.VMEM((TILE, TILE), F32),
                dma((3,)),
            ],
            compiler_params=pltpu.CompilerParams(vmem_limit_bytes=16 * 1024 * 1024),
        )(*(pltpu.with_memory_space_constraint(array, pltpu.VMEM) for array in held))
    )


def solution(mesh):
    split_rows = P(("col", "row"), None, None, None)
    split_panels = P(None, ("col", "row"), None, None)
    return jax.shard_map(
        body,
        mesh=mesh,
        in_specs=(split_rows, P(("col", "row"), None), split_panels, split_panels, P(), P(), P(), P()),
        out_specs=(split_panels, P(), P()),
        check_vma=False,
    )
```
